1024 devices in a mesh: layer: 16 (over z_lo), row: 8 (over y, z_hi), col: 8 (over x, core).
Axes of the slice: x: 4, y: 4, z: 32 (z_hi: 2, z_lo: 16; z = z_hi * 16 + z_lo), core: 2. Of those that a mesh axis runs over, the one named last changes fastest.
Arguments:
- momentum: bfloat16 [16, 896, 4096], P('layer', ('row', 'col')), may hold values from -1 to 1
Outputs:
- update: bfloat16 [16, 896, 4096], P('layer', 'row', 'col')
The draws below stay inside these ranges and needn't reach their ends.
All inputs are finite; a program needn't handle non-finite values.
Results may differ from the reference program's by a relative error of at most 0.024.
Values may be sent and summed in bfloat16 or wider, within the bound.
No kernel may reach another device: no remote copies, remote signals or barrier semaphores. Data moves between devices by JAX's collectives and lax.ppermute only.
A program may use at most 32 MiB of HBM per device.

```python
import math
import jax
import jax.numpy as jnp
from jax import lax

M = 3584
K = 4096
LAYERS = 4
N_COL = 8


def draw_momentum(key, part):
    key = jax.random.fold_in(key, 11)
    keys = jax.random.split(key, 3)
    shape = (4 * LAYERS, M // 4, K)
    noise = jnp.clip(jax.random.normal(keys[0], shape, jnp.float32), -4.0, 4.0)
    level = 0.65
    lower, upper = (0.8, 1.25)
    spread = level / jnp.sqrt(jnp.float32(M + K))
    row_scale = jnp.exp(jax.random.uniform(keys[1], (4 * LAYERS, M // 4, 1), jnp.float32, jnp.log(lower), jnp.log(upper)))
    col_scale = jnp.exp(jax.random.uniform(keys[2], (LAYERS, 1, 1, K), jnp.float32, jnp.log(lower), jnp.log(upper)))
    col_scale = jnp.broadcast_to(col_scale, (LAYERS, 4, 1, K)).reshape(4 * LAYERS, 1, K)
    return (noise * spread * row_scale * col_scale).astype(jnp.bfloat16)


def setup_inputs(seed: int = 0) -> dict:
    key_of = jax.random.split(jax.random.key(seed), 2)
    return {
        "momentum": draw_momentum(jax.random.fold_in(key_of[1], 71), 0),
    }


def reference(momentum):
    results = []
    width = K // N_COL
    root = math.sqrt(max(M, K))
    for layer in range(LAYERS):
        whole = momentum[4 * layer:4 * layer + 4].reshape(M, K)
        gram = jnp.zeros((M, M), jnp.float32)
        for block in range(N_COL):
            piece = whole[:, block * width:(block + 1) * width]
            term = lax.dot_general(piece, piece, (((1,), (1,)), ((), ())), preferred_element_type=jnp.float32)
            term = lax.optimization_barrier(term.astype(jnp.bfloat16))
            gram = gram + term.astype(jnp.float32)
        scaled = gram.astype(jnp.bfloat16)
        first = jnp.dot(scaled, whole, preferred_element_type=jnp.float32).astype(jnp.bfloat16)
        second = jnp.dot(scaled, first, preferred_element_type=jnp.float32)
        mixed = 3.4445 * whole.astype(jnp.float32) - 4.775 * first.astype(jnp.float32) + 2.0315 * second
        results.append((root * mixed).astype(jnp.bfloat16).reshape(4, M // 4, K))
    return jnp.concatenate(results, 0)
```

```python
import math

import jax
import jax.numpy as jnp
from jax import lax
from jax.sharding import Mesh, PartitionSpec as P

AXES = ("layer", "quarter", "y", "half", "x", "core")
SWAP = [(0, 1), (1, 0)]
A1, A2, A3 = 3.4445, -4.775, 2.0315


def dot(lhs, rhs, dims):
    return lax.dot_general(lhs, rhs, (dims, ((), ())), preferred_element_type=jnp.float32)


def total(blocks):
    return jnp.sum(blocks.astype(jnp.float32), 0)


def exchange(blocks, axis):
    return lax.all_to_all(blocks, axis, 0, 0, tiled=True)


def shards(momentum):
    bf16 = jnp.bfloat16
    _, m, k = momentum.shape
    nx, ny, nq, nc = 4, 4, 4, 2
    w = k // nx
    n = nx * m
    own = exchange(momentum[0].reshape(m, nx, w).transpose(1, 0, 2), "x").reshape(n, w)
    other = lax.ppermute(own, "half", SWAP)
    both = jnp.stack([own, other])
    left = lax.all_gather(both, "y", axis=0).reshape(ny * 2 * n, w)
    right = lax.all_gather(both, "quarter", axis=1)
    right = lax.all_gather(right, "core", axis=2).reshape(2 * nq * nc * n, w)
    term = dot(left, right, ((1,), (1,))).astype(bf16)
    mine = total(exchange(term.reshape(nx, 2 * n, 16 * n), "x")).astype(bf16)
    gram = lax.all_gather(mine, "x", axis=0, tiled=True)
    term = dot(gram, right, ((1,), (0,))).astype(bf16)
    first = total(exchange(term.reshape(ny, 2 * n, w), "y")).astype(bf16)
    firsts = lax.all_gather(first, "y", axis=0, tiled=True)
    second = dot(gram[:, : 8 * n], firsts, ((0,), (0,))).reshape(nq, nc, n, w)
    here = (jnp.arange(nq) == lax.axis_index("quarter"))[:, None] & (
        jnp.arange(nc) == lax.axis_index("core")
    )[None]
    pick = jnp.where(here, jnp.float32(A2 / A3), 0.0)[:, :, None, None]
    second = second + pick * first[:n].astype(jnp.float32)[None, None]
    second = second.reshape(nq, nc * n, w)
    core = lax.axis_index("core")
    h = w // 2
    low, high = second[..., :h], second[..., h:]
    keep = jnp.where(core == 0, low, high)
    send = jnp.where(core == 0, high, low).astype(bf16)
    got = lax.ppermute(send, "core", SWAP)
    part = (keep + got.astype(jnp.float32)).astype(bf16)
    second = total(exchange(part, "quarter"))
    tile = lax.dynamic_slice(
        right.reshape(2, nq, nc * n, w), (0, lax.axis_index("quarter"), 0, core * h), (1, 1, nc * n, h)
    )[0, 0]
    mixed = math.sqrt(max(256 * m, k)) * (A1 * tile.astype(jnp.float32) + A3 * second)
    mixed = mixed.reshape(nc, nx, m, h).transpose(1, 0, 2, 3).reshape(nc * n, h)
    return mixed.astype(bf16)[None]


def solution(mesh):
    fine = Mesh(mesh.devices.reshape(-1, 4, 4, 2, 4, 2), AXES)
    return jax.shard_map(
        shards,
        mesh=fine,
        in_specs=(P(("layer", "quarter"), ("y", "half", "x", "core"), None),),
        out_specs=P(("layer", "quarter"), ("y", "half"), ("x", "core")),
        check_vma=False,
    )
```

```python
import math

import jax
import jax.numpy as jnp
from jax import lax
from jax.sharding import Mesh, PartitionSpec as P

AXES = ("layer", "quarter", "y", "half", "x", "core")
SWAP = [(0, 1), (1, 0)]
A1, A2, A3 = 3.4445, -4.775, 2.0315


def dot(lhs, rhs, dims):
    return lax.dot_general(lhs, rhs, (dims, ((), ())), preferred_element_type=jnp.float32)


def total(blocks):
    return jnp.sum(blocks.astype(jnp.float32), 0)


def exchange(blocks, axis):
    return lax.all_to_all(blocks, axis, 0, 0, tiled=True)


def shards(momentum):
    bf16 = jnp.bfloat16
    _, m, k = momentum.shape
    nx, ny, nq, nc = 4, 4, 4, 2
    w = k // nx
    n = nx * m
    own = exchange(momentum[0].reshape(m, nx, w).transpose(1, 0, 2), "x").reshape(n, w)
    other = lax.ppermute(own, "half", SWAP)
    core = lax.axis_index("core")

    def gathered(rows):
        column = lax.all_gather(rows, "quarter", axis=0)
        across = lax.ppermute(column, "core", SWAP)
        line = lax.all_gather(rows, "y", axis=0)
        pair = [jnp.where(core == 0, column, across), jnp.where(core == 0, across, column)]
        return line, jnp.stack(pair, 1)

    own_line, own_block = gathered(own)
    other_line, other_block = gathered(other)
    left = jnp.stack([own_line, other_line], 1).reshape(ny * 2 * n, w)
    right = jnp.stack([own_block, other_block]).reshape(2 * nq * nc * n, w)
    term = dot(left, right, ((1,), (1,))).astype(bf16)
    mine = total(exchange(term.reshape(nx, 2 * n, 16 * n), "x")).astype(bf16)
    gram = lax.all_gather(mine, "x", axis=0, tiled=True)
    term = dot(gram, right, ((1,), (0,))).astype(bf16)
    first = total(exchange(term.reshape(ny, 2 * n, w), "y")).astype(bf16)
    firsts = lax.all_gather(first, "y", axis=0, tiled=True)
    second = dot(gram[:, : 8 * n], firsts, ((0,), (0,))).reshape(nq, nc, n, w)
    here = (jnp.arange(nq) == lax.axis_index("quarter"))[:, None] & (
        jnp.arange(nc) == lax.axis_index("core")
    )[None]
    pick = jnp.where(here, jnp.float32(A2 / A3), 0.0)[:, :, None, None]
    second = second + pick * first[:n].astype(jnp.float32)[None, None]
    second = second.reshape(nq, nc * n, w)
    h = w // 2
    low, high = second[..., :h], second[..., h:]
    keep = jnp.where(core == 0, low, high)
    send = jnp.where(core == 0, high, low).astype(bf16)
    got = lax.ppermute(send, "core", SWAP)
    part = (keep + got.astype(jnp.float32)).astype(bf16)
    second = total(exchange(part, "quarter"))
    tile = lax.dynamic_slice(
        right.reshape(2, nq, nc * n, w), (0, lax.axis_index("quarter"), 0, core * h), (1, 1, nc * n, h)
    )[0, 0]
    mixed = math.sqrt(max(256 * m, k)) * (A1 * tile.astype(jnp.float32) + A3 * second)
    mixed = mixed.reshape(nc, nx, m, h).transpose(1, 0, 2, 3).reshape(nc * n, h)
    return mixed.astype(bf16)[None]


def solution(mesh):
    fine = Mesh(mesh.devices.reshape(-1, 4, 4, 2, 4, 2), AXES)
    return jax.shard_map(
        shards,
        mesh=fine,
        in_specs=(P(("layer", "quarter"), ("y", "half", "x", "core"), None),),
        out_specs=P(("layer", "quarter"), ("y", "half"), ("x", "core")),
        check_vma=False,
    )
```

```python
import math

import jax
import jax.numpy as jnp
from jax import lax
from jax.sharding import Mesh, PartitionSpec as P

AXES = ("layer", "quarter", "y", "half", "x", "core")
SWAP = [(0, 1), (1, 0)]
A1, A2, A3 = 3.4445, -4.775, 2.0315


def dot(lhs, rhs, dims):
    return lax.dot_general(lhs, rhs, (dims, ((), ())), preferred_element_type=jnp.float32)


def total(blocks):
    return jnp.sum(blocks.astype(jnp.float32), 0)


def exchange(blocks, axis):
    return lax.all_to_all(blocks, axis, 0, 0, tiled=True)


def spread(block, axis):
    copies = jnp.broadcast_to(block[None], (4,) + block.shape)
    return exchange(copies, axis)


def ordered(core, mine, other):
    return jnp.where(core == 0, mine, other), jnp.where(core == 0, other, mine)


def shards(momentum):
    bf16 = jnp.bfloat16
    _, m, k = momentum.shape
    nx, ny, nq, nc = 4, 4, 4, 2
    w = k // nx
    h = w // 2
    n = nx * m
    core = lax.axis_index("core")
    own = exchange(momentum[0].reshape(m, nx, w).transpose(1, 0, 2), "x").reshape(n, w)
    other = lax.ppermute(own, "half", SWAP)

    both = jnp.stack([own, other])
    block = spread(both, "quarter")
    left = lax.all_gather(both, "y", axis=0).reshape(ny * 2 * n, w)
    block, left = lax.optimization_barrier((block, left))
    block = jnp.stack(ordered(core, block, lax.ppermute(block, "core", SWAP)), 2)
    right = block.transpose(1, 0, 2, 3, 4).reshape(2 * nq * nc * n, w)

    term = dot(left, right, ((1,), (1,))).astype(bf16)
    mine = total(exchange(term.reshape(nx, 2 * n, 16 * n), "x")).astype(bf16)
    gram = lax.all_gather(mine, "x", axis=0, tiled=True)
    narrow = gram[:, : 8 * n]
    narrow = jnp.concatenate([narrow, lax.ppermute(narrow, "core", SWAP)], 0)

    term = dot(gram, right, ((1,), (0,))).astype(bf16)
    first = total(exchange(term.reshape(ny, 2 * n, w), "y")).astype(bf16)
    keep, send = ordered(core, first[:, :h], first[:, h:])
    first = jnp.stack([keep, lax.ppermute(send, "core", SWAP)])
    firsts = lax.all_gather(first, "y", axis=1).reshape(nc * ny * 2 * n, h)

    term = dot(narrow, firsts, ((0,), (0,))).astype(bf16)
    second = total(exchange(term.reshape(nq, nc * n, h), "quarter"))
    first = jnp.concatenate(ordered(core, first[0, :n], first[1, :n]), 0)
    tile = lax.dynamic_slice(
        right.reshape(2 * nq, nc * n, w), (lax.axis_index("quarter"), 0, core * h), (1, nc * n, h)
    )[0]
    mixed = A1 * tile.astype(jnp.float32) + A2 * first.astype(jnp.float32) + A3 * second
    mixed = math.sqrt(max(256 * m, k)) * mixed
    mixed = mixed.reshape(nc, nx, m, h).transpose(1, 0, 2, 3).reshape(nc * n, h)
    return mixed.astype(bf16)[None]


def solution(mesh):
    fine = Mesh(mesh.devices.reshape(-1, 4, 4, 2, 4, 2), AXES)
    return jax.shard_map(
        shards,
        mesh=fine,
        in_specs=(P(("layer", "quarter"), ("y", "half", "x", "core"), None),),
        out_specs=P(("layer", "quarter"), ("y", "half"), ("x", "core")),
        check_vma=False,
    )
```

```python
import math

import jax
import jax.numpy as jnp
from jax import lax
from jax.sharding import Mesh, PartitionSpec as P

AXES = ("layer", "quarter", "y", "half", "x", "core")
SWAP = [(0, 1), (1, 0)]
A1, A2, A3 = 3.4445, -4.775, 2.0315


def dot(lhs, rhs, dims):
    return lax.dot_general(lhs, rhs, (dims, ((), ())), preferred_element_type=jnp.float32)


def total(blocks):
    return jnp.sum(blocks.astype(jnp.float32), 0)


def exchange(blocks, axis):
    return lax.all_to_all(blocks, axis, 0, 0, tiled=True)


def spread(block, axis):
    copies = jnp.broadcast_to(block[None], (4,) + block.shape)
    return exchange(copies, axis)


def ordered(core, mine, other):
    return jnp.where(core == 0, mine, other), jnp.where(core == 0, other, mine)


def shards(momentum):
    bf16 = jnp.bfloat16
    _, m, k = momentum.shape
    nx, ny, nq, nc = 4, 4, 4, 2
    w = k // nx
    h = w // 2
    n = nx * m
    core = lax.axis_index("core")
    rows = momentum[0].reshape(m, nx, w).transpose(1, 0, 2)
    rows = exchange(jnp.concatenate([rows, rows], 0), ("half", "x")).reshape(2, n, w)
    both = jnp.stack(ordered(lax.axis_index("half"), rows[0], rows[1]))
    block = spread(both, "quarter")
    left = lax.all_gather(both, "y", axis=0).reshape(ny * 2 * n, w)
    block, left = lax.optimization_barrier((block, left))
    block = jnp.stack(ordered(core, block, lax.ppermute(block, "core", SWAP)), 2)
    right = block.transpose(1, 0, 2, 3, 4).reshape(2 * nq * nc * n, w)

    term = dot(left, right, ((1,), (1,))).astype(bf16)
    mine = total(exchange(term.reshape(nx, 2 * n, 16 * n), "x")).astype(bf16)
    gram = lax.all_gather(mine, "x", axis=0, tiled=True)
    narrow = gram[:, : 8 * n]
    narrow = jnp.concatenate([narrow, lax.ppermute(narrow, "core", SWAP)], 0)

    term = dot(gram, right, ((1,), (0,))).astype(bf16)
    first = total(exchange(term.reshape(ny, 2 * n, w), "y")).astype(bf16)
    keep, send = ordered(core, first[:, :h], first[:, h:])
    first = jnp.stack([keep, lax.ppermute(send, "core", SWAP)])
    firsts = lax.all_gather(first, "y", axis=1).reshape(nc * ny * 2 * n, h)

    term = dot(narrow, firsts, ((0,), (0,))).astype(bf16)
    second = total(exchange(term.reshape(nq, nc * n, h), "quarter"))
    first = jnp.concatenate(ordered(core, first[0, :n], first[1, :n]), 0)
    tile = lax.dynamic_slice(
        right.reshape(2 * nq, nc * n, w), (lax.axis_index("quarter"), 0, core * h), (1, nc * n, h)
    )[0]
    mixed = A1 * tile.astype(jnp.float32) + A2 * first.astype(jnp.float32) + A3 * second
    mixed = math.sqrt(max(256 * m, k)) * mixed
    mixed = mixed.reshape(nc, nx, m, h).transpose(1, 0, 2, 3).reshape(nc * n, h)
    return mixed.astype(bf16)[None]


def solution(mesh):
    fine = Mesh(mesh.devices.reshape(-1, 4, 4, 2, 4, 2), AXES)
    return jax.shard_map(
        shards,
        mesh=fine,
        in_specs=(P(("layer", "quarter"), ("y", "half", "x", "core"), None),),
        out_specs=P(("layer", "quarter"), ("y", "half"), ("x", "core")),
        check_vma=False,
    )
```

```python
import math

import jax
import jax.numpy as jnp
from jax import lax
from jax.sharding import Mesh, PartitionSpec as P

AXES = ("layer", "quarter", "y", "half", "x", "core")
SWAP = [(0, 1), (1, 0)]
A1, A2, A3 = 3.4445, -4.775, 2.0315


def dot(lhs, rhs, dims):
    return lax.dot_general(lhs, rhs, (dims, ((), ())), preferred_element_type=jnp.float32)


def total(blocks):
    return jnp.sum(blocks.astype(jnp.float32), 0)


def exchange(blocks, axis):
    return lax.all_to_all(blocks, axis, 0, 0, tiled=True)


def spread(block, axis):
    copies = jnp.broadcast_to(block[None], (4,) + block.shape)
    return exchange(copies, axis)


def ordered(core, mine, other):
    return jnp.where(core == 0, mine, other), jnp.where(core == 0, other, mine)


def shards(momentum):
    bf16 = jnp.bfloat16
    _, m, k = momentum.shape
    nx, ny, nq, nc = 4, 4, 4, 2
    w = k // nx
    h = w // 2
    n = nx * m
    core = lax.axis_index("core")
    own = exchange(momentum[0].reshape(m, nx, w).transpose(1, 0, 2), "x").reshape(n, w)
    other = lax.ppermute(own, "half", SWAP)

    both = jnp.stack([own, other])
    block = spread(both, "quarter")
    left = lax.all_gather(both, "y", axis=0).reshape(ny * 2 * n, w)
    block, left = lax.optimization_barrier((block, left))
    block = jnp.stack(ordered(core, block, lax.ppermute(block, "core", SWAP)), 2)
    right = block.transpose(1, 0, 2, 3, 4).reshape(2 * nq * nc * n, w)

    term = dot(left, right, ((1,), (1,))).astype(bf16)
    mine = total(exchange(term.reshape(nx, 2 * n, 16 * n), "x")).astype(bf16)
    gram = spread(mine, "x").reshape(nx * 2 * n, 16 * n)
    narrow = gram[:, : 8 * n]
    narrow = jnp.stack([narrow.reshape(ny, 2 * n, 8 * n), lax.ppermute(narrow, "core", SWAP).reshape(ny, 2 * n, 8 * n)], 1)
    narrow = narrow.reshape(ny * nc * 2 * n, 8 * n)

    term = dot(gram, right, ((1,), (0,))).astype(bf16)
    terms, narrow = lax.optimization_barrier((exchange(term.reshape(ny, 2 * n, w), "y"), narrow))
    keep, send = ordered(core, terms[..., :h], terms[..., h:])
    send = lax.ppermute(total(send).astype(bf16), "core", SWAP)
    first = jnp.stack([total(keep).astype(bf16), send])
    firsts = spread(first, "y").reshape(nc * ny * 2 * n, h)

    term = dot(narrow, firsts, ((0,), (0,))).astype(bf16)
    second = total(exchange(term.reshape(nq, nc * n, h), "quarter"))
    first = jnp.concatenate(ordered(core, first[0, :n], first[1, :n]), 0)
    tile = lax.dynamic_slice(
        right.reshape(2 * nq, nc * n, w), (lax.axis_index("quarter"), 0, core * h), (1, nc * n, h)
    )[0]
    mixed = A1 * tile.astype(jnp.float32) + A2 * first.astype(jnp.float32) + A3 * second
    mixed = math.sqrt(max(256 * m, k)) * mixed
    mixed = mixed.reshape(nc, nx, m, h).transpose(1, 0, 2, 3).reshape(nc * n, h)
    return mixed.astype(bf16)[None]


def solution(mesh):
    fine = Mesh(mesh.devices.reshape(-1, 4, 4, 2, 4, 2), AXES)
    return jax.shard_map(
        shards,
        mesh=fine,
        in_specs=(P(("layer", "quarter"), ("y", "half", "x", "core"), None),),
        out_specs=P(("layer", "quarter"), ("y", "half"), ("x", "core")),
        check_vma=False,
    )
```

```python
import math

import jax
import jax.numpy as jnp
from jax import lax
from jax.sharding import Mesh, PartitionSpec as P

AXES = ("layer", "quarter", "y", "half", "x", "core")
SWAP = [(0, 1), (1, 0)]
A1, A2, A3 = 3.4445, -4.775, 2.0315


def dot(lhs, rhs, dims):
    return lax.dot_general(lhs, rhs, (dims, ((), ())), preferred_element_type=jnp.float32)


def total(blocks):
    return jnp.sum(blocks.astype(jnp.float32), 0)


def exchange(blocks, axis):
    return lax.all_to_all(blocks, axis, 0, 0, tiled=True)


def spread(block, axis):
    copies = jnp.broadcast_to(block[None], (4,) + block.shape)
    return exchange(copies, axis)


def ordered(core, mine, other):
    return jnp.where(core == 0, mine, other), jnp.where(core == 0, other, mine)


def shards(momentum):
    bf16 = jnp.bfloat16
    _, m, k = momentum.shape
    nx, ny, nq, nc = 4, 4, 4, 2
    w = k // nx
    h = w // 2
    n = nx * m
    core = lax.axis_index("core")
    own = exchange(momentum[0].reshape(m, nx, w).transpose(1, 0, 2), "x").reshape(n, w)
    other = lax.ppermute(own, "half", SWAP)

    both = jnp.stack([own, other])

    right = spread(both, "quarter").transpose(1, 0, 2, 3).reshape(2 * nq * n, w)
    line = lax.all_gather(both.reshape(2 * n, w), "y", axis=0)
    left = jnp.stack(ordered(core, line, lax.ppermute(line, "core", SWAP)), 1)
    left = left.reshape(ny * nc * 2 * n, w)

    term = dot(right, left, ((1,), (1,))).astype(bf16)
    mine = total(exchange(term.reshape(nx, 2 * n, 16 * n), "x")).astype(bf16)
    gram = lax.all_gather(mine, "x", axis=0, tiled=True)
    narrow = gram[: nq * n].reshape(nq, n, 16 * n)
    narrow = jnp.stack(ordered(core, narrow, lax.ppermute(narrow, "core", SWAP)), 1)
    narrow = narrow.reshape(nq * nc * n, 16 * n)

    keep, send = ordered(core, right[:, :h], right[:, h:])
    send = dot(gram, send, ((0,), (0,))).astype(bf16)
    got = lax.ppermute(send, "core", SWAP)
    keep = dot(gram, keep, ((0,), (0,)))
    term = (keep + got.astype(jnp.float32)).astype(bf16)
    term, narrow = lax.optimization_barrier((exchange(term.reshape(ny, 4 * n, h), "y"), narrow))
    first = total(term).astype(bf16)
    firsts = lax.all_gather(first, "y", axis=0, tiled=True)

    term = dot(narrow, firsts, ((1,), (0,))).astype(bf16)
    second = total(exchange(term.reshape(nq, nc * n, h), "quarter"))
    first = first.reshape(nc, 2, n, h)[:, 0].reshape(nc * n, h)
    tile = lax.dynamic_index_in_dim(left.reshape(ny, nc, 2, n, w), lax.axis_index("y"), 0, False)
    tile = tile[:, 0].reshape(nc * n, w)
    tile = jnp.where(core == 0, tile[:, :h], tile[:, h:])
    mixed = A1 * tile.astype(jnp.float32) + A2 * first.astype(jnp.float32) + A3 * second
    mixed = math.sqrt(max(256 * m, k)) * mixed
    mixed = mixed.reshape(nc, nx, m, h).transpose(1, 0, 2, 3).reshape(nc * n, h)
    return mixed.astype(bf16)[None]


def solution(mesh):
    fine = Mesh(mesh.devices.reshape(-1, 4, 4, 2, 4, 2), AXES)
    return jax.shard_map(
        shards,
        mesh=fine,
        in_specs=(P(("layer", "quarter"), ("y", "half", "x", "core"), None),),
        out_specs=P(("layer", "quarter"), ("y", "half"), ("x", "core")),
        check_vma=False,
    )
```

```python
import math

import jax
import jax.numpy as jnp
from jax import lax
from jax.sharding import Mesh, PartitionSpec as P

AXES = ("layer", "quarter", "y", "half", "x", "core")
SWAP = [(0, 1), (1, 0)]
A1, A2, A3 = 3.4445, -4.775, 2.0315


def dot(lhs, rhs, dims):
    return lax.dot_general(lhs, rhs, (dims, ((), ())), preferred_element_type=jnp.float32)


def total(blocks):
    return jnp.sum(blocks.astype(jnp.float32), 0)


def exchange(blocks, axis):
    return lax.all_to_all(blocks, axis, 0, 0, tiled=True)


def spread(block, axis):
    copies = jnp.broadcast_to(block[None], (4,) + block.shape)
    return exchange(copies, axis)


def ordered(core, mine, other):
    return jnp.where(core == 0, mine, other), jnp.where(core == 0, other, mine)


def shards(momentum):
    bf16 = jnp.bfloat16
    _, m, k = momentum.shape
    nx, ny, nq, nc = 4, 4, 4, 2
    w = k // nx
    h = w // 2
    n = nx * m
    core = lax.axis_index("core")
    own = exchange(momentum[0].reshape(m, nx, w).transpose(1, 0, 2), "x").reshape(n, w)
    other = lax.ppermute(own, "half", SWAP)

    both = jnp.stack([own, other])
    block = spread(both, "quarter")
    left = lax.all_gather(both, "y", axis=0).reshape(ny * 2 * n, w)
    block, left = lax.optimization_barrier((block, left))
    block = jnp.stack(ordered(core, block, lax.ppermute(block, "core", SWAP)), 2)
    right = block.transpose(1, 0, 2, 3, 4).reshape(2 * nq * nc * n, w)

    term = dot(left, right, ((1,), (1,))).astype(bf16)
    mine = total(exchange(term.reshape(nx, 2 * n, 16 * n), "x")).astype(bf16)
    gram = lax.all_gather(mine, "x", axis=0, tiled=True)
    narrow = gram[:, : 8 * n]
    narrow = jnp.stack([narrow.reshape(ny, 2 * n, 8 * n), lax.ppermute(narrow, "core", SWAP).reshape(ny, 2 * n, 8 * n)], 1)
    narrow = narrow.reshape(ny * nc * 2 * n, 8 * n)

    term = dot(gram, right, ((1,), (0,))).astype(bf16)
    terms, narrow = lax.optimization_barrier((exchange(term.reshape(ny, 2 * n, w), "y"), narrow))
    keep, send = ordered(core, terms[..., :h], terms[..., h:])
    send = lax.ppermute(total(send).astype(bf16), "core", SWAP)
    first = jnp.stack([total(keep).astype(bf16), send])
    firsts = lax.all_gather(first, "y", axis=0).reshape(ny * nc * 2 * n, h)

    term = dot(narrow, firsts, ((0,), (0,))).astype(bf16)
    second = total(exchange(term.reshape(nq, nc * n, h), "quarter"))
    first = jnp.concatenate(ordered(core, first[0, :n], first[1, :n]), 0)
    tile = lax.dynamic_slice(
        right.reshape(2 * nq, nc * n, w), (lax.axis_index("quarter"), 0, core * h), (1, nc * n, h)
    )[0]
    mixed = A1 * tile.astype(jnp.float32) + A2 * first.astype(jnp.float32) + A3 * second
    mixed = math.sqrt(max(256 * m, k)) * mixed
    mixed = mixed.reshape(nc, nx, m, h).transpose(1, 0, 2, 3).reshape(nc * n, h)
    return mixed.astype(bf16)[None]


def solution(mesh):
    fine = Mesh(mesh.devices.reshape(-1, 4, 4, 2, 4, 2), AXES)
    return jax.shard_map(
        shards,
        mesh=fine,
        in_specs=(P(("layer", "quarter"), ("y", "half", "x", "core"), None),),
        out_specs=P(("layer", "quarter"), ("y", "half"), ("x", "core")),
        check_vma=False,
    )
```

```python
import math

import jax
import jax.numpy as jnp
from jax import lax
from jax.sharding import Mesh, PartitionSpec as P

AXES = ("layer", "quarter", "y", "half", "x", "core")
SWAP = [(0, 1), (1, 0)]
A1, A2, A3 = 3.4445, -4.775, 2.0315


def dot(lhs, rhs, dims):
    return lax.dot_general(lhs, rhs, (dims, ((), ())), preferred_element_type=jnp.float32)


def total(blocks):
    return jnp.sum(blocks.astype(jnp.float32), 0)


def exchange(blocks, axis):
    return lax.all_to_all(blocks, axis, 0, 0, tiled=True)


def spread(block, axis):
    copies = jnp.broadcast_to(block[None], (4,) + block.shape)
    return exchange(copies, axis)


def ordered(core, mine, other):
    return jnp.where(core == 0, mine, other), jnp.where(core == 0, other, mine)


def shards(momentum):
    bf16 = jnp.bfloat16
    _, m, k = momentum.shape
    nx, ny, nq, nc = 4, 4, 4, 2
    w = k // nx
    h = w // 2
    n = nx * m
    core = lax.axis_index("core")
    own = exchange(momentum[0].reshape(m, nx, w).transpose(1, 0, 2), "x").reshape(n, w)
    up = lax.ppermute(own, "half", [(0, 1)])
    down = lax.ppermute(own, "half", [(1, 0)])
    other = jnp.where(lax.axis_index("half") == 1, up, down)

    both = jnp.stack([own, other])
    block = spread(both, "quarter")
    left = lax.all_gather(both, "y", axis=0).reshape(ny * 2 * n, w)
    block, left = lax.optimization_barrier((block, left))
    block = jnp.stack(ordered(core, block, lax.ppermute(block, "core", SWAP)), 2)
    right = block.transpose(1, 0, 2, 3, 4).reshape(2 * nq * nc * n, w)

    term = dot(left, right, ((1,), (1,))).astype(bf16)
    mine = total(exchange(term.reshape(nx, 2 * n, 16 * n), "x")).astype(bf16)
    gram = lax.all_gather(mine, "x", axis=0, tiled=True)
    narrow = gram[:, : 8 * n]
    narrow = jnp.stack([narrow.reshape(ny, 2 * n, 8 * n), lax.ppermute(narrow, "core", SWAP).reshape(ny, 2 * n, 8 * n)], 1)
    narrow = narrow.reshape(ny * nc * 2 * n, 8 * n)

    term = dot(gram, right, ((1,), (0,))).astype(bf16)
    terms, narrow = lax.optimization_barrier((exchange(term.reshape(ny, 2 * n, w), "y"), narrow))
    keep, send = ordered(core, terms[..., :h], terms[..., h:])
    send = lax.ppermute(total(send).astype(bf16), "core", SWAP)
    first = jnp.stack([total(keep).astype(bf16), send])
    firsts = lax.all_gather(first, "y", axis=0).reshape(ny * nc * 2 * n, h)

    term = dot(narrow, firsts, ((0,), (0,))).astype(bf16)
    second = total(exchange(term.reshape(nq, nc * n, h), "quarter"))
    first = jnp.concatenate(ordered(core, first[0, :n], first[1, :n]), 0)
    tile = lax.dynamic_slice(
        right.reshape(2 * nq, nc * n, w), (lax.axis_index("quarter"), 0, core * h), (1, nc * n, h)
    )[0]
    mixed = A1 * tile.astype(jnp.float32) + A2 * first.astype(jnp.float32) + A3 * second
    mixed = math.sqrt(max(256 * m, k)) * mixed
    mixed = mixed.reshape(nc, nx, m, h).transpose(1, 0, 2, 3).reshape(nc * n, h)
    return mixed.astype(bf16)[None]


def solution(mesh):
    fine = Mesh(mesh.devices.reshape(-1, 4, 4, 2, 4, 2), AXES)
    return jax.shard_map(
        shards,
        mesh=fine,
        in_specs=(P(("layer", "quarter"), ("y", "half", "x", "core"), None),),
        out_specs=P(("layer", "quarter"), ("y", "half"), ("x", "core")),
        check_vma=False,
    )
```

```python
import math

import jax
import jax.numpy as jnp
from jax import lax
from jax.sharding import Mesh, PartitionSpec as P

AXES = ("layer", "quarter", "y", "half", "x", "core")
SWAP = [(0, 1), (1, 0)]
A1, A2, A3 = 3.4445, -4.775, 2.0315


def dot(lhs, rhs, dims):
    return lax.dot_general(lhs, rhs, (dims, ((), ())), preferred_element_type=jnp.float32)


def total(blocks):
    return jnp.sum(blocks.astype(jnp.float32), 0)


def exchange(blocks, axis):
    return lax.all_to_all(blocks, axis, 0, 0, tiled=True)


def spread(block, axis):
    copies = jnp.broadcast_to(block[None], (4,) + block.shape)
    return exchange(copies, axis)


def ordered(core, mine, other):
    return jnp.where(core == 0, mine, other), jnp.where(core == 0, other, mine)


def shards(momentum):
    bf16 = jnp.bfloat16
    _, m, k = momentum.shape
    nx, ny, nq, nc = 4, 4, 4, 2
    w = k // nx
    h = w // 2
    n = nx * m
    core = lax.axis_index("core")
    rows = jnp.stack([momentum[0, :, i * w : (i + 1) * w] for i in range(nx)])
    own = exchange(rows, "x").reshape(n, w)
    other = lax.ppermute(own, "half", SWAP)

    both = jnp.stack([own, other])
    block = spread(both, "quarter")
    left = lax.all_gather(both, "y", axis=0).reshape(ny * 2 * n, w)
    block, left = lax.optimization_barrier((block, left))
    block = jnp.stack(ordered(core, block, lax.ppermute(block, "core", SWAP)), 2)
    right = block.transpose(1, 0, 2, 3, 4).reshape(2 * nq * nc * n, w)

    term = dot(left, right, ((1,), (1,))).astype(bf16)
    mine = total(exchange(term.reshape(nx, 2 * n, 16 * n), "x")).astype(bf16)
    gram = lax.all_gather(mine, "x", axis=0, tiled=True)
    narrow = gram[:, : 8 * n]
    narrow = jnp.concatenate([narrow, lax.ppermute(narrow, "core", SWAP)], 0)

    term = dot(gram, right, ((1,), (0,))).astype(bf16)
    terms = exchange(term.reshape(ny, 2 * n, w), "y")
    keep, send = ordered(core, terms[..., :h], terms[..., h:])
    send = lax.ppermute(total(send).astype(bf16), "core", SWAP)
    first = jnp.stack([total(keep).astype(bf16), send])
    firsts = lax.all_gather(first, "y", axis=1).reshape(nc * ny * 2 * n, h)

    term = dot(narrow, firsts, ((0,), (0,))).astype(bf16)
    second = total(exchange(term.reshape(nq, nc * n, h), "quarter"))
    first = jnp.concatenate(ordered(core, first[0, :n], first[1, :n]), 0)
    tile = lax.dynamic_slice(
        right.reshape(2 * nq, nc * n, w), (lax.axis_index("quarter"), 0, core * h), (1, nc * n, h)
    )[0]
    mixed = A1 * tile.astype(jnp.float32) + A2 * first.astype(jnp.float32) + A3 * second
    mixed = math.sqrt(max(256 * m, k)) * mixed
    mixed = mixed.reshape(nc, nx, m, h).transpose(1, 0, 2, 3).reshape(nc * n, h)
    return mixed.astype(bf16)[None]


def solution(mesh):
    fine = Mesh(mesh.devices.reshape(-1, 4, 4, 2, 4, 2), AXES)
    return jax.shard_map(
        shards,
        mesh=fine,
        in_specs=(P(("layer", "quarter"), ("y", "half", "x", "core"), None),),
        out_specs=P(("layer", "quarter"), ("y", "half"), ("x", "core")),
        check_vma=False,
    )
```

```python
import math

import jax
import jax.numpy as jnp
from jax import lax
from jax.sharding import Mesh, PartitionSpec as P

AXES = ("layer", "quarter", "y", "half", "x", "core")
SWAP = [(0, 1), (1, 0)]
A1, A2, A3 = 3.4445, -4.775, 2.0315


def dot(lhs, rhs, dims):
    return lax.dot_general(lhs, rhs, (dims, ((), ())), preferred_element_type=jnp.float32)


def total(blocks):
    return jnp.sum(blocks.astype(jnp.float32), 0)


def exchange(blocks, axis):
    return lax.all_to_all(blocks, axis, 0, 0, tiled=True)


def spread(block, axis):
    copies = jnp.broadcast_to(block[None], (4,) + block.shape)
    return exchange(copies, axis)


def ordered(core, mine, other):
    return jnp.where(core == 0, mine, other), jnp.where(core == 0, other, mine)


def shards(momentum):
    bf16 = jnp.bfloat16
    _, m, k = momentum.shape
    nx, ny, nq, nc = 4, 4, 4, 2
    w = k // nx
    h = w // 2
    n = nx * m
    core = lax.axis_index("core")
    rows = jnp.stack([momentum[0, :, i * w : (i + 1) * w] for i in range(nx)])
    x = lax.axis_index("x")
    got = []
    for step in range(nx):
        block = lax.dynamic_index_in_dim(rows, (x + step) % nx, 0, False)
        pairs = [(g * nx + i, (1 - g) * nx + (i + step) % nx) for g in range(2) for i in range(nx)]
        got.append(lax.ppermute(block, ("half", "x"), pairs))
    got = jnp.stack(got)
    other = jnp.concatenate([lax.dynamic_index_in_dim(got, (x - i) % nx, 0, False) for i in range(nx)], 0)
    own = exchange(rows, "x").reshape(n, w)
    both = jnp.stack([own, other])
    block = spread(both, "quarter")
    left = lax.all_gather(both, "y", axis=0).reshape(ny * 2 * n, w)
    block, left = lax.optimization_barrier((block, left))
    block = jnp.stack(ordered(core, block, lax.ppermute(block, "core", SWAP)), 2)
    right = block.transpose(1, 0, 2, 3, 4).reshape(2 * nq * nc * n, w)

    term = dot(left, right, ((1,), (1,))).astype(bf16)
    mine = total(exchange(term.reshape(nx, 2 * n, 16 * n), "x")).astype(bf16)
    gram = lax.all_gather(mine, "x", axis=0, tiled=True)
    narrow = gram[:, : 8 * n]
    narrow = jnp.concatenate([narrow, lax.ppermute(narrow, "core", SWAP)], 0)

    term = dot(gram, right, ((1,), (0,))).astype(bf16)
    terms = exchange(term.reshape(ny, 2 * n, w), "y")
    keep, send = ordered(core, terms[..., :h], terms[..., h:])
    send = lax.ppermute(total(send).astype(bf16), "core", SWAP)
    first = jnp.stack([total(keep).astype(bf16), send])
    firsts = lax.all_gather(first, "y", axis=1).reshape(nc * ny * 2 * n, h)

    term = dot(narrow, firsts, ((0,), (0,))).astype(bf16)
    second = total(exchange(term.reshape(nq, nc * n, h), "quarter"))
    first = jnp.concatenate(ordered(core, first[0, :n], first[1, :n]), 0)
    tile = lax.dynamic_slice(
        right.reshape(2 * nq, nc * n, w), (lax.axis_index("quarter"), 0, core * h), (1, nc * n, h)
    )[0]
    mixed = A1 * tile.astype(jnp.float32) + A2 * first.astype(jnp.float32) + A3 * second
    mixed = math.sqrt(max(256 * m, k)) * mixed
    mixed = mixed.reshape(nc, nx, m, h).transpose(1, 0, 2, 3).reshape(nc * n, h)
    return mixed.astype(bf16)[None]


def solution(mesh):
    fine = Mesh(mesh.devices.reshape(-1, 4, 4, 2, 4, 2), AXES)
    return jax.shard_map(
        shards,
        mesh=fine,
        in_specs=(P(("layer", "quarter"), ("y", "half", "x", "core"), None),),
        out_specs=P(("layer", "quarter"), ("y", "half"), ("x", "core")),
        check_vma=False,
    )
```

```python
import math

import jax
import jax.numpy as jnp
from jax import lax
from jax.sharding import Mesh, PartitionSpec as P

AXES = ("layer", "quarter", "y", "half", "x", "core")
SWAP = [(0, 1), (1, 0)]
A1, A2, A3 = 3.4445, -4.775, 2.0315


def dot(lhs, rhs, dims):
    return lax.dot_general(lhs, rhs, (dims, ((), ())), preferred_element_type=jnp.float32)


def total(blocks):
    return jnp.sum(blocks.astype(jnp.float32), 0)


def exchange(blocks, axis):
    return lax.all_to_all(blocks, axis, 0, 0, tiled=True)


def spread(block, axis):
    copies = jnp.broadcast_to(block[None], (4,) + block.shape)
    return exchange(copies, axis)


def ordered(core, mine, other):
    return jnp.where(core == 0, mine, other), jnp.where(core == 0, other, mine)


def shards(momentum):
    bf16 = jnp.bfloat16
    _, m, k = momentum.shape
    nx, ny, nq, nc = 4, 4, 4, 2
    w = k // nx
    h = w // 2
    n = nx * m
    core = lax.axis_index("core")
    rows = jnp.stack([momentum[0, :, i * w : (i + 1) * w] for i in range(nx)])
    own = exchange(rows, "x").reshape(n, w)
    other = lax.ppermute(own, "half", SWAP)

    both = jnp.stack([own, other])
    block = spread(both.reshape(2 * n, w), "quarter").reshape(nq, 2, n, w)
    left = lax.all_gather(both, "y", axis=0).reshape(ny * 2 * n, w)
    block, left = lax.optimization_barrier((block, left))
    block = jnp.stack(ordered(core, block, lax.ppermute(block, "core", SWAP)), 2)
    right = block.transpose(1, 0, 2, 3, 4).reshape(2 * nq * nc * n, w)

    term = dot(left, right, ((1,), (1,))).astype(bf16)
    mine = total(exchange(term.reshape(nx, 2 * n, 16 * n), "x")).astype(bf16)
    gram = spread(mine, "x").reshape(nx * 2 * n, 16 * n)
    narrow = gram[:, : 8 * n]
    narrow = jnp.concatenate([narrow, lax.ppermute(narrow, "core", SWAP)], 0)

    term = dot(gram, right, ((1,), (0,))).astype(bf16)
    terms = exchange(term.reshape(ny, 2 * n, w), "y")
    keep, send = ordered(core, terms[..., :h], terms[..., h:])
    send = lax.ppermute(total(send).astype(bf16), "core", SWAP)
    first = jnp.stack([total(keep).astype(bf16), send])
    firsts = spread(first.reshape(nc * 2 * n, h), "y").reshape(ny, nc, 2 * n, h)
    firsts = firsts.transpose(1, 0, 2, 3).reshape(nc * ny * 2 * n, h)

    term = dot(narrow, firsts, ((0,), (0,))).astype(bf16)
    second = total(exchange(term.reshape(nq, nc * n, h), "quarter"))
    first = jnp.concatenate(ordered(core, first[0, :n], first[1, :n]), 0)
    tile = lax.dynamic_slice(
        right.reshape(2 * nq, nc * n, w), (lax.axis_index("quarter"), 0, core * h), (1, nc * n, h)
    )[0]
    mixed = A1 * tile.astype(jnp.float32) + A2 * first.astype(jnp.float32) + A3 * second
    mixed = math.sqrt(max(256 * m, k)) * mixed
    mixed = mixed.reshape(nc, nx, m, h).transpose(1, 0, 2, 3).reshape(nc * n, h)
    return mixed.astype(bf16)[None]


def solution(mesh):
    fine = Mesh(mesh.devices.reshape(-1, 4, 4, 2, 4, 2), AXES)
    return jax.shard_map(
        shards,
        mesh=fine,
        in_specs=(P(("layer", "quarter"), ("y", "half", "x", "core"), None),),
        out_specs=P(("layer", "quarter"), ("y", "half"), ("x", "core")),
        check_vma=False,
    )
```

```python
import math

import jax
import jax.numpy as jnp
from jax import lax
from jax.sharding import Mesh, PartitionSpec as P

AXES = ("layer", "quarter", "y", "half", "x", "core")
SWAP = [(0, 1), (1, 0)]
A1, A2, A3 = 3.4445, -4.775, 2.0315


def dot(lhs, rhs, dims):
    return lax.dot_general(lhs, rhs, (dims, ((), ())), preferred_element_type=jnp.float32)


def total(blocks):
    return jnp.sum(blocks.astype(jnp.float32), 0)


def exchange(blocks, axis):
    return lax.all_to_all(blocks, axis, 0, 0, tiled=True)


def spread(block, axis):
    copies = jnp.broadcast_to(block[None], (4,) + block.shape)
    return exchange(copies, axis)


def ordered(core, mine, other):
    return jnp.where(core == 0, mine, other), jnp.where(core == 0, other, mine)


def shards(momentum):
    bf16 = jnp.bfloat16
    _, m, k = momentum.shape
    nx, ny, nq, nc = 4, 4, 4, 2
    w = k // nx
    h = w // 2
    n = nx * m
    core = lax.axis_index("core")
    rows = jnp.stack([momentum[0, :, i * w : (i + 1) * w] for i in range(nx)])
    own = exchange(rows, "x").reshape(n, w)
    other = lax.ppermute(own, "half", SWAP)


    early = lax.all_gather(own, "y", axis=0)
    early, other = lax.optimization_barrier((early, other))
    line = jnp.stack([early, lax.all_gather(other, "y", axis=0)])
    left = jnp.stack(ordered(core, line, lax.ppermute(line, "core", SWAP)), 1)
    tile = lax.dynamic_index_in_dim(left[0], lax.axis_index("y"), 1, False).reshape(nc * n, w)
    left = left.reshape(2 * nc * ny * n, w)
    right = spread(jnp.concatenate([own, other], 0), "quarter").reshape(nq, 2, n, w)
    right = right.transpose(1, 0, 2, 3).reshape(2 * nq * n, w)

    term = dot(right, left, ((1,), (1,))).astype(bf16)
    mine = total(exchange(term.reshape(nx, 2 * n, 16 * n), "x")).astype(bf16)
    gram = lax.all_gather(mine, "x", axis=0, tiled=True)
    narrow = gram[: nq * n].reshape(nq, n, 16 * n)
    narrow = jnp.stack(ordered(core, narrow, lax.ppermute(narrow, "core", SWAP)), 1)
    narrow = narrow.reshape(nq * nc * n, 16 * n)

    keep, send = ordered(core, right[:, :h], right[:, h:])
    send = dot(gram, send, ((0,), (0,))).astype(bf16)
    got = lax.ppermute(send, "core", SWAP)
    keep = dot(gram, keep, ((0,), (0,)))
    term = (keep + got.astype(jnp.float32)).astype(bf16)
    term = term.reshape(2 * nc, ny, n, h).transpose(1, 0, 2, 3).reshape(ny, 4 * n, h)
    term, narrow = lax.optimization_barrier((exchange(term, "y"), narrow))
    first = total(term).astype(bf16)
    firsts = lax.all_gather(first.reshape(2 * nc, n, h), "y", axis=1).reshape(16 * n, h)

    term = dot(narrow, firsts, ((1,), (0,))).astype(bf16)
    second = total(exchange(term.reshape(nq, nc * n, h), "quarter"))
    first = first[: nc * n]
    tile = jnp.where(core == 0, tile[:, :h], tile[:, h:])
    mixed = A1 * tile.astype(jnp.float32) + A2 * first.astype(jnp.float32) + A3 * second
    mixed = math.sqrt(max(256 * m, k)) * mixed
    mixed = mixed.reshape(nc, nx, m, h).transpose(1, 0, 2, 3).reshape(nc * n, h)
    return mixed.astype(bf16)[None]


def solution(mesh):
    fine = Mesh(mesh.devices.reshape(-1, 4, 4, 2, 4, 2), AXES)
    return jax.shard_map(
        shards,
        mesh=fine,
        in_specs=(P(("layer", "quarter"), ("y", "half", "x", "core"), None),),
        out_specs=P(("layer", "quarter"), ("y", "half"), ("x", "core")),
        check_vma=False,
    )
```

```python
import math

import jax
import jax.numpy as jnp
from jax import lax
from jax.sharding import Mesh, PartitionSpec as P

AXES = ("layer", "quarter", "y", "half", "x", "core")
SWAP = [(0, 1), (1, 0)]
A1, A2, A3 = 3.4445, -4.775, 2.0315


def dot(lhs, rhs, dims):
    return lax.dot_general(lhs, rhs, (dims, ((), ())), preferred_element_type=jnp.float32)


def total(blocks):
    return jnp.sum(blocks.astype(jnp.float32), 0)


def exchange(blocks, axis):
    return lax.all_to_all(blocks, axis, 0, 0, tiled=True)


def spread(block, axis):
    copies = jnp.broadcast_to(block[None], (4,) + block.shape)
    return exchange(copies, axis)


def ordered(core, mine, other):
    return jnp.where(core == 0, mine, other), jnp.where(core == 0, other, mine)


def half_pairs(layers):
    return [(2 * i + g, 2 * i + 1 - g) for i in layers for g in range(2)]


def shards(momentum):
    bf16 = jnp.bfloat16
    _, m, k = momentum.shape
    nx, ny, nq, nc = 4, 4, 4, 2
    w = k // nx
    h = w // 2
    n = nx * m
    core = lax.axis_index("core")
    rows = jnp.stack([momentum[0, :, i * w : (i + 1) * w] for i in range(nx)])
    layers = lax.axis_size("layer")
    early = lax.ppermute(rows, ("layer", "half"), half_pairs(range(layers // 2)))
    own = exchange(rows, "x").reshape(n, w)
    late = lax.ppermute(own, ("layer", "half"), half_pairs(range(layers // 2, layers)))
    early = exchange(early, "x").reshape(n, w)
    other = jnp.where(lax.axis_index("layer") < layers // 2, early, late)

    both = jnp.stack([own, other])
    block = spread(both, "quarter")
    left = lax.all_gather(both, "y", axis=0).reshape(ny * 2 * n, w)
    block, left = lax.optimization_barrier((block, left))
    block = jnp.stack(ordered(core, block, lax.ppermute(block, "core", SWAP)), 2)
    right = block.transpose(1, 0, 2, 3, 4).reshape(2 * nq * nc * n, w)

    term = dot(left, right, ((1,), (1,))).astype(bf16)
    mine = total(exchange(term.reshape(nx, 2 * n, 16 * n), "x")).astype(bf16)
    gram = lax.all_gather(mine, "x", axis=0, tiled=True)
    narrow = gram[:, : 8 * n]
    narrow = jnp.concatenate([narrow, lax.ppermute(narrow, "core", SWAP)], 0)

    term = dot(gram, right, ((1,), (0,))).astype(bf16)
    terms = exchange(term.reshape(ny, 2 * n, w), "y")
    keep, send = ordered(core, terms[..., :h], terms[..., h:])
    send = lax.ppermute(total(send).astype(bf16), "core", SWAP)
    first = jnp.stack([total(keep).astype(bf16), send])
    firsts = lax.all_gather(first, "y", axis=1).reshape(nc * ny * 2 * n, h)

    term = dot(narrow, firsts, ((0,), (0,))).astype(bf16)
    second = total(exchange(term.reshape(nq, nc * n, h), "quarter"))
    first = jnp.concatenate(ordered(core, first[0, :n], first[1, :n]), 0)
    tile = lax.dynamic_slice(
        right.reshape(2 * nq, nc * n, w), (lax.axis_index("quarter"), 0, core * h), (1, nc * n, h)
    )[0]
    mixed = A1 * tile.astype(jnp.float32) + A2 * first.astype(jnp.float32) + A3 * second
    mixed = math.sqrt(max(256 * m, k)) * mixed
    mixed = mixed.reshape(nc, nx, m, h).transpose(1, 0, 2, 3).reshape(nc * n, h)
    return mixed.astype(bf16)[None]


def solution(mesh):
    fine = Mesh(mesh.devices.reshape(-1, 4, 4, 2, 4, 2), AXES)
    return jax.shard_map(
        shards,
        mesh=fine,
        in_specs=(P(("layer", "quarter"), ("y", "half", "x", "core"), None),),
        out_specs=P(("layer", "quarter"), ("y", "half"), ("x", "core")),
        check_vma=False,
    )
```

```python
import math

import jax
import jax.numpy as jnp
from jax import lax
from jax.sharding import Mesh, PartitionSpec as P

AXES = ("layer", "quarter", "y", "half", "x", "core")
SWAP = [(0, 1), (1, 0)]
A1, A2, A3 = 3.4445, -4.775, 2.0315


def dot(lhs, rhs, dims):
    return lax.dot_general(lhs, rhs, (dims, ((), ())), preferred_element_type=jnp.float32)


def total(blocks):
    return jnp.sum(blocks.astype(jnp.float32), 0)


def exchange(blocks, axis):
    return lax.all_to_all(blocks, axis, 0, 0, tiled=True)


def spread(block, axis):
    copies = jnp.broadcast_to(block[None], (4,) + block.shape)
    return exchange(copies, axis)


def ordered(core, mine, other):
    return jnp.where(core == 0, mine, other), jnp.where(core == 0, other, mine)


def half_pairs(layers):
    return [(2 * i + g, 2 * i + 1 - g) for i in layers for g in range(2)]


def shards(momentum):
    bf16 = jnp.bfloat16
    _, m, k = momentum.shape
    nx, ny, nq, nc = 4, 4, 4, 2
    w = k // nx
    h = w // 2
    n = nx * m
    core = lax.axis_index("core")
    rows = jnp.stack([momentum[0, :, i * w : (i + 1) * w] for i in range(nx)])
    layers = lax.axis_size("layer")
    early = lax.ppermute(rows, ("layer", "half"), half_pairs(range(layers // 4)))
    own = exchange(rows, "x").reshape(n, w)
    late = lax.ppermute(own, ("layer", "half"), half_pairs(range(layers // 4, layers)))
    early = exchange(early, "x").reshape(n, w)
    other = jnp.where(lax.axis_index("layer") < layers // 4, early, late)

    both = jnp.stack([own, other])
    block = spread(both, "quarter")
    left = lax.all_gather(both, "y", axis=0).reshape(ny * 2 * n, w)
    block, left = lax.optimization_barrier((block, left))
    block = jnp.stack(ordered(core, block, lax.ppermute(block, "core", SWAP)), 2)
    right = block.transpose(1, 0, 2, 3, 4).reshape(2 * nq * nc * n, w)

    term = dot(left, right, ((1,), (1,))).astype(bf16)
    mine = total(exchange(term.reshape(nx, 2 * n, 16 * n), "x")).astype(bf16)
    gram = lax.all_gather(mine, "x", axis=0, tiled=True)
    narrow = gram[:, : 8 * n]
    narrow = jnp.concatenate([narrow, lax.ppermute(narrow, "core", SWAP)], 0)

    term = dot(gram, right, ((1,), (0,))).astype(bf16)
    terms = exchange(term.reshape(ny, 2 * n, w), "y")
    keep, send = ordered(core, terms[..., :h], terms[..., h:])
    send = lax.ppermute(total(send).astype(bf16), "core", SWAP)
    first = jnp.stack([total(keep).astype(bf16), send])
    firsts = lax.all_gather(first, "y", axis=1).reshape(nc * ny * 2 * n, h)

    term = dot(narrow, firsts, ((0,), (0,))).astype(bf16)
    second = total(exchange(term.reshape(nq, nc * n, h), "quarter"))
    first = jnp.concatenate(ordered(core, first[0, :n], first[1, :n]), 0)
    tile = lax.dynamic_slice(
        right.reshape(2 * nq, nc * n, w), (lax.axis_index("quarter"), 0, core * h), (1, nc * n, h)
    )[0]
    mixed = A1 * tile.astype(jnp.float32) + A2 * first.astype(jnp.float32) + A3 * second
    mixed = math.sqrt(max(256 * m, k)) * mixed
    mixed = mixed.reshape(nc, nx, m, h).transpose(1, 0, 2, 3).reshape(nc * n, h)
    return mixed.astype(bf16)[None]


def solution(mesh):
    fine = Mesh(mesh.devices.reshape(-1, 4, 4, 2, 4, 2), AXES)
    return jax.shard_map(
        shards,
        mesh=fine,
        in_specs=(P(("layer", "quarter"), ("y", "half", "x", "core"), None),),
        out_specs=P(("layer", "quarter"), ("y", "half"), ("x", "core")),
        check_vma=False,
    )
```

```python
import math

import jax
import jax.numpy as jnp
from jax import lax
from jax.sharding import Mesh, PartitionSpec as P

AXES = ("layer", "quarter", "y", "half", "x", "core")
SWAP = [(0, 1), (1, 0)]
A1, A2, A3 = 3.4445, -4.775, 2.0315


def dot(lhs, rhs, dims):
    return lax.dot_general(lhs, rhs, (dims, ((), ())), preferred_element_type=jnp.float32)


def total(blocks):
    return jnp.sum(blocks.astype(jnp.float32), 0)


def exchange(blocks, axis):
    return lax.all_to_all(blocks, axis, 0, 0, tiled=True)


def spread(block, axis):
    copies = jnp.broadcast_to(block[None], (4,) + block.shape)
    return exchange(copies, axis)


def ordered(core, mine, other):
    return jnp.where(core == 0, mine, other), jnp.where(core == 0, other, mine)


def shards(momentum):
    bf16 = jnp.bfloat16
    _, m, k = momentum.shape
    nx, ny, nq, nc = 4, 4, 4, 2
    w = k // nx
    h = w // 2
    n = nx * m
    core = lax.axis_index("core")
    rows = jnp.stack([momentum[0, :, i * w : (i + 1) * w] for i in range(nx)])
    own = exchange(rows, "x").reshape(n, w)
    crossed = [(2 * q + g, 2 * (q ^ 1) + 1 - g) for q in range(nq) for g in range(2)]
    other = lax.ppermute(own, ("quarter", "half"), crossed)

    both = jnp.stack([own, other])
    block = spread(both, "quarter")
    left = lax.all_gather(both, "y", axis=0).reshape(ny * 2 * n, w)
    block, left = lax.optimization_barrier((block, left))
    block = jnp.stack(ordered(core, block, lax.ppermute(block, "core", SWAP)), 2)
    right = block.transpose(1, 0, 2, 3, 4).reshape(2 * nq * nc * n, w)

    term = dot(left, right, ((1,), (1,))).astype(bf16)
    mine = total(exchange(term.reshape(nx, 2 * n, 16 * n), "x")).astype(bf16)
    gram = lax.all_gather(mine, "x", axis=0, tiled=True)
    narrow = gram[:, : 8 * n]
    narrow = jnp.concatenate([narrow, lax.ppermute(narrow, "core", SWAP)], 0)

    term = dot(gram, right, ((1,), (0,))).astype(bf16)
    terms = exchange(term.reshape(ny, 2 * n, w), "y")
    keep, send = ordered(core, terms[..., :h], terms[..., h:])
    send = lax.ppermute(total(send).astype(bf16), "core", SWAP)
    first = jnp.stack([total(keep).astype(bf16), send])
    firsts = lax.all_gather(first, "y", axis=1).reshape(nc * ny * 2 * n, h)

    term = dot(narrow, firsts, ((0,), (0,))).astype(bf16)
    second = total(exchange(term.reshape(nq, nc * n, h), "quarter"))
    first = jnp.concatenate(ordered(core, first[0, :n], first[1, :n]), 0)
    tile = lax.dynamic_slice(
        right.reshape(2 * nq, nc * n, w), (lax.axis_index("quarter"), 0, core * h), (1, nc * n, h)
    )[0]
    mixed = A1 * tile.astype(jnp.float32) + A2 * first.astype(jnp.float32) + A3 * second
    mixed = math.sqrt(max(256 * m, k)) * mixed
    mixed = mixed.reshape(nc, nx, m, h).transpose(1, 0, 2, 3).reshape(nc * n, h)
    return mixed.astype(bf16)[None]


def solution(mesh):
    fine = Mesh(mesh.devices.reshape(-1, 4, 4, 2, 4, 2), AXES)
    return jax.shard_map(
        shards,
        mesh=fine,
        in_specs=(P(("layer", "quarter"), ("y", "half", "x", "core"), None),),
        out_specs=P(("layer", "quarter"), ("y", "half"), ("x", "core")),
        check_vma=False,
    )
```

```python
import math

import jax
import jax.numpy as jnp
from jax import lax
from jax.sharding import Mesh, PartitionSpec as P

AXES = ("layer", "quarter", "y", "half", "x", "core")
SWAP = [(0, 1), (1, 0)]
A1, A2, A3 = 3.4445, -4.775, 2.0315


def dot(lhs, rhs, dims):
    return lax.dot_general(lhs, rhs, (dims, ((), ())), preferred_element_type=jnp.float32)


def total(blocks):
    return jnp.sum(blocks.astype(jnp.float32), 0)


def exchange(blocks, axis):
    return lax.all_to_all(blocks, axis, 0, 0, tiled=True)


def spread(block, axis):
    copies = jnp.broadcast_to(block[None], (4,) + block.shape)
    return exchange(copies, axis)


def ordered(core, mine, other):
    return jnp.where(core == 0, mine, other), jnp.where(core == 0, other, mine)


def shards(momentum):
    bf16 = jnp.bfloat16
    _, m, k = momentum.shape
    nx, ny, nq, nc = 4, 4, 4, 2
    w = k // nx
    h = w // 2
    n = nx * m
    core = lax.axis_index("core")
    rows = jnp.stack([momentum[0, :, i * w : (i + 1) * w] for i in range(nx)])
    own = exchange(rows, "x").reshape(n, w)
    other = lax.ppermute(own, "half", SWAP)
    own_block = spread(own, "quarter")
    other_block = spread(other, "quarter")
    left = lax.all_gather(jnp.stack([own, other]), "y", axis=0).reshape(ny * 2 * n, w)
    other_block, left = lax.optimization_barrier((other_block, left))
    right = []
    for block in (own_block, other_block):
        right.append(jnp.stack(ordered(core, block, lax.ppermute(block, "core", SWAP)), 1))
    right = jnp.stack(right).reshape(2 * nq * nc * n, w)

    term = dot(left, right, ((1,), (1,))).astype(bf16)
    mine = total(exchange(term.reshape(nx, 2 * n, 16 * n), "x")).astype(bf16)
    gram = lax.all_gather(mine, "x", axis=0, tiled=True)
    narrow = gram[:, : 8 * n]
    narrow = jnp.concatenate([narrow, lax.ppermute(narrow, "core", SWAP)], 0)

    term = dot(gram, right, ((1,), (0,))).astype(bf16)
    terms = exchange(term.reshape(ny, 2 * n, w), "y")
    keep, send = ordered(core, terms[..., :h], terms[..., h:])
    send = lax.ppermute(total(send).astype(bf16), "core", SWAP)
    first = jnp.stack([total(keep).astype(bf16), send])
    firsts = lax.all_gather(first, "y", axis=1).reshape(nc * ny * 2 * n, h)

    term = dot(narrow, firsts, ((0,), (0,))).astype(bf16)
    second = total(exchange(term.reshape(nq, nc * n, h), "quarter"))
    first = jnp.concatenate(ordered(core, first[0, :n], first[1, :n]), 0)
    tile = lax.dynamic_slice(
        right.reshape(2 * nq, nc * n, w), (lax.axis_index("quarter"), 0, core * h), (1, nc * n, h)
    )[0]
    mixed = A1 * tile.astype(jnp.float32) + A2 * first.astype(jnp.float32) + A3 * second
    mixed = math.sqrt(max(256 * m, k)) * mixed
    mixed = mixed.reshape(nc, nx, m, h).transpose(1, 0, 2, 3).reshape(nc * n, h)
    return mixed.astype(bf16)[None]


def solution(mesh):
    fine = Mesh(mesh.devices.reshape(-1, 4, 4, 2, 4, 2), AXES)
    return jax.shard_map(
        shards,
        mesh=fine,
        in_specs=(P(("layer", "quarter"), ("y", "half", "x", "core"), None),),
        out_specs=P(("layer", "quarter"), ("y", "half"), ("x", "core")),
        check_vma=False,
    )
```

```python
import math

import jax
import jax.numpy as jnp
from jax import lax
from jax.sharding import Mesh, PartitionSpec as P

AXES = ("layer", "quarter", "y", "half", "x", "core")
SWAP = [(0, 1), (1, 0)]
A1, A2, A3 = 3.4445, -4.775, 2.0315


def dot(lhs, rhs, dims):
    return lax.dot_general(lhs, rhs, (dims, ((), ())), preferred_element_type=jnp.float32)


def total(blocks):
    return jnp.sum(blocks.astype(jnp.float32), 0)


def exchange(blocks, axis):
    return lax.all_to_all(blocks, axis, 0, 0, tiled=True)


def spread(block, axis):
    copies = jnp.broadcast_to(block[None], (4,) + block.shape)
    return exchange(copies, axis)


def ordered(core, mine, other):
    return jnp.where(core == 0, mine, other), jnp.where(core == 0, other, mine)


def shards(momentum):
    bf16 = jnp.bfloat16
    _, m, k = momentum.shape
    nx, ny, nq, nc = 4, 4, 4, 2
    w = k // nx
    h = w // 2
    n = nx * m
    core = lax.axis_index("core")
    rows = jnp.stack([momentum[0, :, i * w : (i + 1) * w] for i in range(nx)])
    own = exchange(rows, "x").reshape(n, w)
    other = lax.ppermute(own, "half", SWAP)

    both = jnp.stack([own, other])
    block = spread(both, "quarter")
    left = lax.all_gather(both, "y", axis=0).reshape(ny * 2 * n, w)
    block, left = lax.optimization_barrier((block, left))
    across = lax.ppermute(block, "core", SWAP)
    right = jnp.stack([jnp.stack(ordered(core, block[:, g], across[:, g]), 1) for g in range(2)])
    right = right.reshape(2 * nq * nc * n, w)

    term = dot(left, right, ((1,), (1,))).astype(bf16)
    mine = total(exchange(term.reshape(nx, 2 * n, 16 * n), "x")).astype(bf16)
    gram = lax.all_gather(mine, "x", axis=0, tiled=True)
    narrow = gram[:, : 8 * n]
    narrow = jnp.concatenate([narrow, lax.ppermute(narrow, "core", SWAP)], 0)

    term = dot(gram, right, ((1,), (0,))).astype(bf16)
    terms = exchange(term.reshape(ny, 2 * n, w), "y")
    keep, send = ordered(core, terms[..., :h], terms[..., h:])
    send = lax.ppermute(total(send).astype(bf16), "core", SWAP)
    first = jnp.stack([total(keep).astype(bf16), send])
    firsts = lax.all_gather(first, "y", axis=1).reshape(nc * ny * 2 * n, h)

    term = dot(narrow, firsts, ((0,), (0,))).astype(bf16)
    second = total(exchange(term.reshape(nq, nc * n, h), "quarter"))
    first = jnp.concatenate(ordered(core, first[0, :n], first[1, :n]), 0)
    tile = lax.dynamic_slice(
        right.reshape(2 * nq, nc * n, w), (lax.axis_index("quarter"), 0, core * h), (1, nc * n, h)
    )[0]
    mixed = A1 * tile.astype(jnp.float32) + A2 * first.astype(jnp.float32) + A3 * second
    mixed = math.sqrt(max(256 * m, k)) * mixed
    mixed = mixed.reshape(nc, nx, m, h).transpose(1, 0, 2, 3).reshape(nc * n, h)
    return mixed.astype(bf16)[None]


def solution(mesh):
    fine = Mesh(mesh.devices.reshape(-1, 4, 4, 2, 4, 2), AXES)
    return jax.shard_map(
        shards,
        mesh=fine,
        in_specs=(P(("layer", "quarter"), ("y", "half", "x", "core"), None),),
        out_specs=P(("layer", "quarter"), ("y", "half"), ("x", "core")),
        check_vma=False,
    )
```

```python
import math

import jax
import jax.numpy as jnp
from jax import lax
from jax.sharding import Mesh, PartitionSpec as P

AXES = ("layer", "quarter", "y", "half", "x", "core")
SWAP = [(0, 1), (1, 0)]
A1, A2, A3 = 3.4445, -4.775, 2.0315


def dot(lhs, rhs, dims):
    return lax.dot_general(lhs, rhs, (dims, ((), ())), preferred_element_type=jnp.float32)


def total(blocks):
    return jnp.sum(blocks.astype(jnp.float32), 0)


def exchange(blocks, axis):
    return lax.all_to_all(blocks, axis, 0, 0, tiled=True)


def spread(block, axis):
    copies = jnp.broadcast_to(block[None], (4,) + block.shape)
    return exchange(copies, axis)


def ordered(core, mine, other):
    return jnp.where(core == 0, mine, other), jnp.where(core == 0, other, mine)


def shards(momentum):
    bf16 = jnp.bfloat16
    _, m, k = momentum.shape
    nx, ny, nq, nc = 4, 4, 4, 2
    w = k // nx
    h = w // 2
    n = nx * m
    core = lax.axis_index("core")
    rows = jnp.stack([momentum[0, :, i * w : (i + 1) * w] for i in range(nx)])
    own = exchange(rows, "x").reshape(n, w)
    other = lax.ppermute(own, "half", SWAP)

    both = jnp.stack([own, other])
    block = spread(both, "quarter")
    left = lax.all_gather(both, "y", axis=0).reshape(ny * 2 * n, w)
    block, left = lax.optimization_barrier((block, left))
    across = lax.ppermute(block, "core", SWAP)
    right = jnp.stack([jnp.stack(ordered(core, block[:, g], across[:, g]), 1) for g in range(2)])
    right = right.reshape(2 * nq * nc * n, w)

    term = dot(left, right, ((1,), (1,))).astype(bf16)
    mine = total(exchange(term.reshape(nx, 2 * n, 16 * n), "x")).astype(bf16)
    gram = lax.all_gather(mine, "x", axis=0, tiled=True)
    term = dot(gram, right, ((1,), (0,))).astype(bf16)
    narrow = gram[:, : 8 * n]
    wide = jnp.pad(narrow, ((0, 0), (0, h - 8 * n)))
    term, wide = lax.optimization_barrier((term, wide))
    terms = exchange(term.reshape(ny, 2 * n, w), "y")
    keep, send = ordered(core, terms[..., :h], terms[..., h:])
    got = lax.ppermute(jnp.concatenate([total(send).astype(bf16), wide], 0), "core", SWAP)
    first = jnp.stack([total(keep).astype(bf16), got[: 2 * n]])
    narrow = jnp.concatenate([narrow, got[2 * n :, : 8 * n]], 0)
    firsts = lax.all_gather(first, "y", axis=1).reshape(nc * ny * 2 * n, h)

    term = dot(narrow, firsts, ((0,), (0,))).astype(bf16)
    second = total(exchange(term.reshape(nq, nc * n, h), "quarter"))
    first = jnp.concatenate(ordered(core, first[0, :n], first[1, :n]), 0)
    tile = lax.dynamic_slice(
        right.reshape(2 * nq, nc * n, w), (lax.axis_index("quarter"), 0, core * h), (1, nc * n, h)
    )[0]
    mixed = A1 * tile.astype(jnp.float32) + A2 * first.astype(jnp.float32) + A3 * second
    mixed = math.sqrt(max(256 * m, k)) * mixed
    mixed = mixed.reshape(nc, nx, m, h).transpose(1, 0, 2, 3).reshape(nc * n, h)
    return mixed.astype(bf16)[None]


def solution(mesh):
    fine = Mesh(mesh.devices.reshape(-1, 4, 4, 2, 4, 2), AXES)
    return jax.shard_map(
        shards,
        mesh=fine,
        in_specs=(P(("layer", "quarter"), ("y", "half", "x", "core"), None),),
        out_specs=P(("layer", "quarter"), ("y", "half"), ("x", "core")),
        check_vma=False,
    )
```

```python
import math

import jax
import jax.numpy as jnp
from jax import lax
from jax.sharding import Mesh, PartitionSpec as P

AXES = ("layer", "quarter", "y", "half", "x", "core")
SWAP = [(0, 1), (1, 0)]
A1, A2, A3 = 3.4445, -4.775, 2.0315


def dot(lhs, rhs, dims):
    return lax.dot_general(lhs, rhs, (dims, ((), ())), preferred_element_type=jnp.float32)


def total(blocks):
    return jnp.sum(blocks.astype(jnp.float32), 0)


def exchange(blocks, axis):
    return lax.all_to_all(blocks, axis, 0, 0, tiled=True)


def spread(block, axis):
    copies = jnp.broadcast_to(block[None], (4,) + block.shape)
    return exchange(copies, axis)


def ordered(core, mine, other):
    return jnp.where(core == 0, mine, other), jnp.where(core == 0, other, mine)


def shards(momentum):
    bf16 = jnp.bfloat16
    _, m, k = momentum.shape
    nx, ny, nq, nc = 4, 4, 4, 2
    w = k // nx
    h = w // 2
    n = nx * m
    core = lax.axis_index("core")
    rows = jnp.stack([momentum[0, :, i * w : (i + 1) * w] for i in range(nx)])
    own = exchange(rows, "x").reshape(n, w)
    other = lax.ppermute(own, "half", SWAP)

    both = jnp.stack([own, other])
    block = spread(both, "quarter")
    left = lax.all_gather(both, "y", axis=0).reshape(ny * 2 * n, w)
    block, left = lax.optimization_barrier((block, left))
    across = lax.ppermute(block, "core", SWAP)
    right = jnp.stack([jnp.stack(ordered(core, block[:, g], across[:, g]), 1) for g in range(2)])
    right = right.reshape(2 * nq * nc * n, w)

    term = dot(left, right, ((1,), (1,))).astype(bf16)
    mine = total(exchange(term.reshape(nx, 2 * n, 16 * n), "x")).astype(bf16)
    gram = lax.all_gather(mine, "x", axis=0, tiled=True)
    term = dot(gram, right, ((1,), (0,))).astype(bf16)
    narrow = gram[:, : 8 * n]
    wide = jnp.pad(narrow, ((0, 0), (0, h - 8 * n)))
    term, wide = lax.optimization_barrier((term, wide))
    terms = exchange(term.reshape(ny, 2 * n, w), "y")
    keep, send = ordered(core, terms[..., :h], terms[..., h:])
    got = lax.ppermute(jnp.concatenate([total(send).astype(bf16), wide], 0), "core", SWAP)
    tile = lax.dynamic_slice(
        right.reshape(2 * nq, nc * n, w), (lax.axis_index("quarter"), 0, core * h), (1, nc * n, h)
    )[0]
    tile, got = lax.optimization_barrier((A1 * tile.astype(jnp.float32), got))
    first = jnp.stack([total(keep).astype(bf16), got[: 2 * n]])
    narrow = jnp.concatenate([narrow, got[2 * n :, : 8 * n]], 0)
    firsts = lax.all_gather(first, "y", axis=1).reshape(nc * ny * 2 * n, h)
    first = jnp.concatenate(ordered(core, first[0, :n], first[1, :n]), 0)
    part = tile + A2 * first.astype(jnp.float32)

    term = dot(narrow, firsts, ((0,), (0,))).astype(bf16)
    term, part = lax.optimization_barrier((term, part))
    second = total(exchange(term.reshape(nq, nc * n, h), "quarter"))
    mixed = math.sqrt(max(256 * m, k)) * (part + A3 * second)
    mixed = mixed.astype(bf16)
    pieces = [mixed[(c * nx + i) * m : (c * nx + i + 1) * m] for i in range(nx) for c in range(nc)]
    return jnp.concatenate(pieces, 0)[None]


def solution(mesh):
    fine = Mesh(mesh.devices.reshape(-1, 4, 4, 2, 4, 2), AXES)
    return jax.shard_map(
        shards,
        mesh=fine,
        in_specs=(P(("layer", "quarter"), ("y", "half", "x", "core"), None),),
        out_specs=P(("layer", "quarter"), ("y", "half"), ("x", "core")),
        check_vma=False,
    )
```

```python
import math

import jax
import jax.numpy as jnp
from jax import lax
from jax.sharding import Mesh, PartitionSpec as P

AXES = ("layer", "quarter", "y", "half", "x", "core")
SWAP = [(0, 1), (1, 0)]
A1, A2, A3 = 3.4445, -4.775, 2.0315


def dot(lhs, rhs, dims):
    return lax.dot_general(lhs, rhs, (dims, ((), ())), preferred_element_type=jnp.float32)


def total(blocks):
    return jnp.sum(blocks.astype(jnp.float32), 0)


def exchange(blocks, axis):
    return lax.all_to_all(blocks, axis, 0, 0, tiled=True)


def spread(block, axis):
    copies = jnp.broadcast_to(block[None], (4,) + block.shape)
    return exchange(copies, axis)


def ordered(core, mine, other):
    return jnp.where(core == 0, mine, other), jnp.where(core == 0, other, mine)


def shards(momentum):
    bf16 = jnp.bfloat16
    _, m, k = momentum.shape
    nx, ny, nq, nc = 4, 4, 4, 2
    w = k // nx
    h = w // 2
    n = nx * m
    core = lax.axis_index("core")
    rows = jnp.stack([momentum[0, :, i * w : (i + 1) * w] for i in range(nx)])
    own = exchange(rows, "x").reshape(n, w)
    other = lax.ppermute(own, "half", SWAP)

    both = jnp.stack([own, other])
    block = spread(both, "quarter")
    left = lax.all_gather(both, "y", axis=0).reshape(ny * 2 * n, w)
    block, left = lax.optimization_barrier((block, left))
    across = lax.ppermute(block, "core", SWAP)
    right = jnp.stack([jnp.stack(ordered(core, block[:, g], across[:, g]), 1) for g in range(2)])
    right = right.reshape(2 * nq * nc * n, w)

    term = dot(left, right, ((1,), (1,))).astype(bf16)
    mine = total(exchange(term.reshape(nx, 2 * n, 16 * n), "x")).astype(bf16)
    gram = lax.all_gather(mine, "x", axis=0, tiled=True)
    narrow = gram[:, : 8 * n]
    narrow = jnp.concatenate([narrow, lax.ppermute(narrow, "core", SWAP)], 0)

    term = dot(gram, right, ((1,), (0,))).astype(bf16)
    terms = exchange(term.reshape(ny, 2 * n, w), "y")
    keep, send = ordered(core, terms[..., :h], terms[..., h:])
    send = lax.ppermute(total(send).astype(bf16), "core", SWAP)
    first = jnp.stack([total(keep).astype(bf16), send])
    firsts = lax.all_gather(first, "y", axis=1).reshape(nc * ny * 2 * n, h)

    first = jnp.concatenate(ordered(core, first[0, :n], first[1, :n]), 0)
    tile = lax.dynamic_slice(
        right.reshape(2 * nq, nc * n, w), (lax.axis_index("quarter"), 0, core * h), (1, nc * n, h)
    )[0]
    part = A1 * tile.astype(jnp.float32) + A2 * first.astype(jnp.float32)

    term = dot(narrow, firsts, ((0,), (0,))).astype(bf16)
    term, part = lax.optimization_barrier((term, part))
    second = total(exchange(term.reshape(nq, nc * n, h), "quarter"))
    mixed = math.sqrt(max(256 * m, k)) * (part + A3 * second)
    mixed = mixed.reshape(nc, nx, m, h).transpose(1, 0, 2, 3).reshape(nc * n, h)
    return mixed.astype(bf16)[None]


def solution(mesh):
    fine = Mesh(mesh.devices.reshape(-1, 4, 4, 2, 4, 2), AXES)
    return jax.shard_map(
        shards,
        mesh=fine,
        in_specs=(P(("layer", "quarter"), ("y", "half", "x", "core"), None),),
        out_specs=P(("layer", "quarter"), ("y", "half"), ("x", "core")),
        check_vma=False,
    )
```

```python
import math

import jax
import jax.numpy as jnp
from jax import lax
from jax.sharding import Mesh, PartitionSpec as P

AXES = ("layer", "quarter", "y", "half", "x", "core")
SWAP = [(0, 1), (1, 0)]
A1, A2, A3 = 3.4445, -4.775, 2.0315


def dot(lhs, rhs, dims):
    return lax.dot_general(lhs, rhs, (dims, ((), ())), preferred_element_type=jnp.float32)


def total(blocks):
    return jnp.sum(blocks.astype(jnp.float32), 0)


def exchange(blocks, axis):
    return lax.all_to_all(blocks, axis, 0, 0, tiled=True)


def spread(block, axis):
    copies = jnp.broadcast_to(block[None], (4,) + block.shape)
    return exchange(copies, axis)


def ordered(core, mine, other):
    return jnp.where(core == 0, mine, other), jnp.where(core == 0, other, mine)


def shards(momentum):
    bf16 = jnp.bfloat16
    _, m, k = momentum.shape
    nx, ny, nq, nc = 4, 4, 4, 2
    w = k // nx
    h = w // 2
    n = nx * m
    core = lax.axis_index("core")
    rows = jnp.stack([momentum[0, :, i * w : (i + 1) * w] for i in range(nx)])
    own = exchange(rows, "x").reshape(n, w)
    crossed = [(2 * q + g, 2 * (q ^ 1) + 1 - g) for q in range(nq) for g in range(2)]
    other = lax.ppermute(own, ("quarter", "half"), crossed)

    both = jnp.stack([own, other])
    block = spread(both, "quarter")
    left = lax.all_gather(both, "y", axis=0).reshape(ny * 2 * n, w)
    block, left = lax.optimization_barrier((block, left))
    across = lax.ppermute(block, "core", SWAP)
    right = jnp.stack([jnp.stack(ordered(core, block[:, g], across[:, g]), 1) for g in range(2)])
    right = right.reshape(2 * nq * nc * n, w)

    term = dot(left, right, ((1,), (1,))).astype(bf16)
    mine = total(exchange(term.reshape(nx, 2 * n, 16 * n), "x")).astype(bf16)
    gram = lax.all_gather(mine, "x", axis=0, tiled=True)
    narrow = gram[:, : 8 * n]
    narrow = jnp.concatenate([narrow, lax.ppermute(narrow, "core", SWAP)], 0)

    term = dot(gram, right, ((1,), (0,))).astype(bf16)
    terms = exchange(term.reshape(ny, 2 * n, w), "y")
    keep, send = ordered(core, terms[..., :h], terms[..., h:])
    send = lax.ppermute(total(send).astype(bf16), "core", SWAP)
    first = jnp.stack([total(keep).astype(bf16), send])
    firsts = lax.all_gather(first, "y", axis=1).reshape(nc * ny * 2 * n, h)

    first = jnp.concatenate(ordered(core, first[0, :n], first[1, :n]), 0)
    tile = lax.dynamic_slice(
        right.reshape(2 * nq, nc * n, w), (lax.axis_index("quarter"), 0, core * h), (1, nc * n, h)
    )[0]
    part = A1 * tile.astype(jnp.float32) + A2 * first.astype(jnp.float32)

    term = dot(narrow, firsts, ((0,), (0,))).astype(bf16)
    term, part = lax.optimization_barrier((term, part))
    second = total(exchange(term.reshape(nq, nc * n, h), "quarter"))
    mixed = math.sqrt(max(256 * m, k)) * (part + A3 * second)
    mixed = mixed.reshape(nc, nx, m, h).transpose(1, 0, 2, 3).reshape(nc * n, h)
    return mixed.astype(bf16)[None]


def solution(mesh):
    fine = Mesh(mesh.devices.reshape(-1, 4, 4, 2, 4, 2), AXES)
    return jax.shard_map(
        shards,
        mesh=fine,
        in_specs=(P(("layer", "quarter"), ("y", "half", "x", "core"), None),),
        out_specs=P(("layer", "quarter"), ("y", "half"), ("x", "core")),
        check_vma=False,
    )
```

```python
import math

import jax
import jax.numpy as jnp
from jax import lax
from jax.sharding import Mesh, PartitionSpec as P

AXES = ("layer", "quarter", "y", "half", "x", "core")
SWAP = [(0, 1), (1, 0)]
A1, A2, A3 = 3.4445, -4.775, 2.0315


def dot(lhs, rhs, dims):
    return lax.dot_general(lhs, rhs, (dims, ((), ())), preferred_element_type=jnp.float32)


def total(blocks):
    return jnp.sum(blocks.astype(jnp.float32), 0)


def exchange(blocks, axis):
    return lax.all_to_all(blocks, axis, 0, 0, tiled=True)


def spread(block, axis):
    copies = jnp.broadcast_to(block[None], (4,) + block.shape)
    return exchange(copies, axis)


def ordered(core, mine, other):
    return jnp.where(core == 0, mine, other), jnp.where(core == 0, other, mine)


def shards(momentum):
    bf16 = jnp.bfloat16
    _, m, k = momentum.shape
    nx, ny, nq, nc = 4, 4, 4, 2
    w = k // nx
    h = w // 2
    n = nx * m
    core = lax.axis_index("core")
    rows = jnp.stack([momentum[0, :, i * w : (i + 1) * w] for i in range(nx)])
    own = exchange(rows, "x").reshape(n, w)
    other = lax.ppermute(own, "half", SWAP)

    both = jnp.stack([own, other])
    block = spread(both.reshape(2 * n, w), "quarter").reshape(nq, 2, n, w)
    left = lax.all_gather(both, "y", axis=0).reshape(ny * 2 * n, w)
    block, left = lax.optimization_barrier((block, left))
    across = lax.ppermute(block, "core", SWAP)
    right = jnp.stack([jnp.stack(ordered(core, block[:, g], across[:, g]), 1) for g in range(2)])
    right = right.reshape(2 * nq * nc * n, w)

    term = dot(left, right, ((1,), (1,))).astype(bf16)
    mine = total(exchange(term.reshape(nx, 2 * n, 16 * n), "x")).astype(bf16)
    gram = lax.all_gather(mine, "x", axis=0, tiled=True)
    narrow = gram[:, : 8 * n]
    narrow = jnp.concatenate([narrow, lax.ppermute(narrow, "core", SWAP)], 0)

    term = dot(gram, right, ((1,), (0,))).astype(bf16)
    terms = exchange(term.reshape(ny, 2 * n, w), "y")
    keep, send = ordered(core, terms[..., :h], terms[..., h:])
    send = lax.ppermute(total(send).astype(bf16), "core", SWAP)
    first = jnp.stack([total(keep).astype(bf16), send])
    firsts = lax.all_gather(first, "y", axis=1).reshape(nc * ny * 2 * n, h)

    first = jnp.concatenate(ordered(core, first[0, :n], first[1, :n]), 0)
    tile = lax.dynamic_slice(
        right.reshape(2 * nq, nc * n, w), (lax.axis_index("quarter"), 0, core * h), (1, nc * n, h)
    )[0]
    part = A1 * tile.astype(jnp.float32) + A2 * first.astype(jnp.float32)

    term = dot(narrow, firsts, ((0,), (0,))).astype(bf16)
    term, part = lax.optimization_barrier((term, part))
    second = total(exchange(term.reshape(nq, nc * n, h), "quarter"))
    mixed = math.sqrt(max(256 * m, k)) * (part + A3 * second)
    mixed = mixed.reshape(nc, nx, m, h).transpose(1, 0, 2, 3).reshape(nc * n, h)
    return mixed.astype(bf16)[None]


def solution(mesh):
    fine = Mesh(mesh.devices.reshape(-1, 4, 4, 2, 4, 2), AXES)
    return jax.shard_map(
        shards,
        mesh=fine,
        in_specs=(P(("layer", "quarter"), ("y", "half", "x", "core"), None),),
        out_specs=P(("layer", "quarter"), ("y", "half"), ("x", "core")),
        check_vma=False,
    )
```
